32 devices in a mesh: groups: 2 (over y), region: 4 (over z), seg: 2 (over x), tb: 2 (over core).
Axes of the slice: x: 2, y: 2, z: 4, core: 2. Of those that a mesh axis runs over, the one named last changes fastest.
Arguments:
- records: bfloat16 [16, 3, 1024], P(('groups', 'region'), None, 'seg'), parts along dimension 0, may hold values from -6 to 6
- templates: bfloat16 [4, 64, 16, 3, 512], P(('groups', 'tb'), None, 'region'), parts along dimension 0, may hold values from -6 to 6
- channel_mask: int32 [4, 64, 16, 3], P(('groups', 'tb'), None, 'region'), parts along dimension 0, may hold values 0 or 1
- station_region: int32 [16], P(('groups', 'region')), parts along dimension 0, may hold values from 0 to 3, as said below
Outputs:
- detect: float32 [4, 64, 1024], P(('groups', 'tb'), None, 'seg'), parts along dimension 0
The draws below stay inside these ranges and needn't reach their ends.
There are 2 independent parts, one for each index of `groups`. The reference program is written for one: setup_inputs(seed, part) draws one part's arguments, and reference() takes and returns one part's arrays. A program takes and returns all parts, laid end to end along the dimension named above; each array names one. Nothing has to cross between parts.
Inputs may be any that keep to these rules, and one draw needn't show every extreme that they name: `station_region`: the 2 stations of one device (aligned blocks of 2 station numbers) name distinct regions. No region is named by more than 4 stations, and one region by exactly 4.
All inputs are finite; a program needn't handle non-finite values. No bound on the sum of `channel_mask` on one device may be relied on, other than what follows from the above.
Results may differ from the reference program's by a relative error of at most 0.0041.
Values may be sent and summed in bfloat16 or wider, within the bound.
A program may use at most 64 MiB of HBM per device.

```python
import jax
import jax.numpy as jnp
from jax import lax

TLEN = 512
K = 64
BATCHES = 2
REGIONS = 4
STA_DEV = 2
STATIONS = 8
CAP = 4
TOTAL_LEN = 1024


def draw_station_region(key, part):
    base_key = jax.random.fold_in(key, 11)
    key_regions, key_roles, key_local = jax.random.split(base_key, 3)
    region_order = jax.random.permutation(key_regions, REGIONS)
    sender_roles = jax.random.permutation(key_roles, REGIONS)
    local_scores = jax.random.randint(key_local, (REGIONS, STA_DEV), 0, 1 << 20) * STA_DEV
    local_scores = local_scores + jnp.arange(STA_DEV, dtype=jnp.int32)[None, :]
    position = jnp.argsort(jnp.argsort(local_scores, axis=1, stable=True), axis=1, stable=True)
    sender_role = sender_roles[:, None]
    cyclic = max(REGIONS - 1, 1)
    heavy_pick = jnp.where(position == 0, 0, (sender_role + position - 1) % cyclic + 1)
    light_pick = (sender_role + position) % cyclic + 1
    chosen = jnp.where(sender_role < CAP, heavy_pick, light_pick)
    return region_order[chosen].reshape(STATIONS).astype(jnp.int32)


def touch_ends(array, own_key, least, largest):
    spot = [jax.random.randint(jax.random.fold_in(own_key, axis), (), 0, length) for axis, length in enumerate(array.shape)]
    widest = array.shape.index(max(array.shape))
    neighbour = spot[:widest] + [(spot[widest] + 1) % array.shape[widest]] + spot[widest + 1:]
    return array.at[tuple(spot)].set(least).at[tuple(neighbour)].set(largest)


def block_levels(key, shape, cuts, low, top_value):
    level = 1.0
    for dim, blocks in cuts:
        heights = jax.random.uniform(jax.random.fold_in(jax.random.fold_in(key, 6), dim), (blocks,), jnp.float32, low / len(cuts), top_value / len(cuts))
        level = level * jnp.repeat(jnp.exp(heights), shape[dim] // blocks).reshape((-1,) + (1,) * (len(shape) - 1 - dim))
    return level


def noise(key, shape, deviation, bound, shards=(), kind=jnp.bfloat16):
    entries = deviation * jax.random.normal(key, shape, jnp.float32)
    if shards:
        entries = entries * block_levels(key, shape, shards, -0.22, 0.18)
    return jnp.clip(entries, -bound, bound).astype(kind)


def setup_inputs(seed: int = 0, part: int = 0) -> dict:
    seeds = jax.random.split(jax.random.key(seed), 5)
    part_keys = jax.random.split(jax.random.fold_in(seeds[4], part), 5)
    records = noise(part_keys[0], (STATIONS, 3, TOTAL_LEN), 1.0, 6.0, ((0, 4), (2, 2)))
    templates = noise(part_keys[1], (BATCHES, K, REGIONS * CAP, 3, TLEN), 1.0, 6.0, ((0, 2), (2, 4)))
    channel_mask = touch_ends((jax.random.randint(part_keys[2], (BATCHES, K, REGIONS * CAP, 3), 0, 4) < 3).astype(jnp.int32), jax.random.fold_in(part_keys[2], 1), 0, 1)
    station_region = draw_station_region(jax.random.fold_in(jax.random.fold_in(seeds[4], part), 71), part)
    return dict(records=records, templates=templates, channel_mask=channel_mask, station_region=station_region)


def window_rows(stretch, columns, filter_taps):
    channels, window_span = stretch.shape
    repeated = jnp.broadcast_to(stretch[:, None, :], (channels, columns + 1, window_span))
    repeated = repeated.reshape(channels, (columns + 1) * window_span)
    shifted = repeated[:, :columns * (window_span + 1)].reshape(channels, columns, window_span + 1)
    return shifted[:, :, :filter_taps]

def scaled_windows(stretch, columns, filter_taps):
    widened = window_rows(stretch, columns, filter_taps).astype(jnp.float32)
    energy = lax.optimization_barrier(jnp.sum(widened * widened, axis=2))
    return (widened / jnp.sqrt(jnp.maximum(energy, 1.0))[:, :, None]).astype(jnp.bfloat16)

def reference(records, templates, channel_mask, station_region):
    stations = records.shape[0]
    total_len = records.shape[2]
    station_ids = jnp.arange(stations, dtype=jnp.int32)
    earlier = (station_region[None, :] == station_region[:, None]) & (station_ids[None, :] < station_ids[:, None])
    slot_ranks = lax.optimization_barrier(jnp.sum(earlier.astype(jnp.int32), axis=1))
    slot_of = station_region * CAP + slot_ranks
    slot_index = jnp.arange(REGIONS * CAP, dtype=jnp.int32)
    placing = slot_index[:, None] == slot_of[None, :]
    owned_rows = jnp.dot(placing.astype(jnp.bfloat16), records.reshape(stations, -1), preferred_element_type=jnp.float32).astype(jnp.bfloat16)
    owned_rows = owned_rows.reshape(REGIONS * CAP, 3, total_len)
    filled = lax.optimization_barrier(jnp.sum(placing.astype(jnp.float32), axis=1))
    padding = jnp.zeros((REGIONS * CAP, 3, TLEN), jnp.bfloat16)
    flat_owned = jnp.concatenate([owned_rows, padding], axis=2).reshape(REGIONS * CAP * 3, total_len + TLEN)
    weight = channel_mask.astype(jnp.float32) * filled[None, None, :, None]
    widened_templates = templates.astype(jnp.float32)
    template_norm = jnp.sqrt(lax.optimization_barrier(jnp.sum(widened_templates * widened_templates, axis=4, keepdims=True)) + 1e-06)
    normed = (widened_templates * weight[..., None] / template_norm).astype(jnp.bfloat16)
    normed_wide = normed.reshape(BATCHES * K, REGIONS * CAP * 3, TLEN).astype(jnp.float32)
    columns = 128

    def one_block(block_index):
        offset = block_index * columns
        stretch = lax.dynamic_slice_in_dim(flat_owned, offset, columns + TLEN - 1, 1)
        scaled = scaled_windows(stretch, columns, TLEN).astype(jnp.float32)
        return jnp.einsum('rct,cut->ru', normed_wide, scaled)
    blocks = lax.map(one_block, jnp.arange(total_len // columns, dtype=jnp.int32))
    stacked = jnp.transpose(blocks, (1, 0, 2)).reshape(BATCHES * K, total_len)
    power_sum = lax.optimization_barrier(jnp.mean(stacked * stacked, axis=1))
    detect = stacked / jnp.sqrt(power_sum + 1e-06)[:, None]
    return detect.reshape(BATCHES, K, total_len)
```

```python
import functools

import jax
import jax.numpy as jnp
from jax import lax
from jax.experimental import pallas as pl
from jax.experimental.pallas import tpu as pltpu
from jax.sharding import PartitionSpec as P

MESH = pl.DeviceIdType.MESH
LANES = 128
ROWS = 16
F32 = jnp.float32
BF16 = jnp.bfloat16


def each(count, body):
    if count <= 8:
        for index in range(count):
            body(index)
    else:
        def step(index, carry):
            body(index)
            return carry

        lax.fori_loop(0, count, step, 0)


def detect_kernel(
    regions,
    segs,
    region_ref,
    rec_ref,
    tmpl_ref,
    mask_ref,
    out_ref,
    station_buf,
    pay_buf,
    got_buf,
    own_buf,
    inv_buf,
    normed_buf,
    hankel_buf,
    part_buf,
    sums_buf,
    mine_buf,
    gather_buf,
    power_mine,
    power_buf,
    pay_send,
    pay_recv,
    part_send,
    part_recv,
    gather_send,
    gather_recv,
    power_send,
    power_recv,
):
    components, local_count, seg_len = rec_ref.shape
    channels, kept, taps = normed_buf.shape
    capacity = channels // components
    pieces = seg_len // LANES
    chunks = part_buf.shape[0]
    total_len = seg_len * segs
    me = lax.axis_index("region")
    seg = lax.axis_index("seg")

    barrier = pltpu.get_barrier_semaphore()

    def greet(index):
        r, s = index // segs, index % segs

        @pl.when((r != me) | (s != seg))
        def _():
            pl.semaphore_signal(barrier, inc=1, device_id={"region": r, "seg": s}, device_id_type=MESH)

    each(regions * segs, greet)

    station_buf[...] = jnp.ones_like(station_buf)
    for c in range(components):
        samples = rec_ref[c].astype(F32)
        for n in range(local_count):
            for j in range(pieces):
                station_buf[n, pl.ds(c * pieces + j, 1), :] = samples[n : n + 1, j * LANES : (j + 1) * LANES]

    def fill(r):
        total = jnp.zeros((ROWS, LANES), F32)
        for n in range(local_count):
            total = total + station_buf[n] * (region_ref[n] == r).astype(F32)
        pay_buf[r] = total.astype(BF16)

    each(regions, fill)
    got_buf[0, me] = pay_buf[me]

    @pl.when(seg == segs - 1)
    def _():
        got_buf[1] = jnp.zeros(got_buf.shape[1:], BF16)

    pl.semaphore_wait(barrier, regions * segs - 1)

    def pay_copy(which, r, slot, target_seg):
        return pltpu.make_async_remote_copy(
            src_ref=pay_buf.at[r],
            dst_ref=got_buf.at[which, slot],
            send_sem=pay_send.at[which, r],
            recv_sem=pay_recv.at[which, slot],
            device_id={"region": r, "seg": target_seg},
            device_id_type=MESH,
        )

    def send_records(r):
        @pl.when(r != me)
        def _():
            pay_copy(0, r, me, seg).start()

        @pl.when(seg > 0)
        def _():
            pay_copy(1, r, me, jnp.maximum(seg - 1, 0)).start()

    each(regions, send_records)

    half = taps // 2
    flip_row = lax.broadcasted_iota(jnp.int32, (half, half), 0)
    flip_col = lax.broadcasted_iota(jnp.int32, (half, half), 1)
    flip = (flip_row + flip_col == half - 1).astype(BF16)
    group_rows = ROWS * channels
    rows_of = lax.broadcasted_iota(jnp.int32, (group_rows, group_rows), 0)
    cols_of = lax.broadcasted_iota(jnp.int32, (group_rows, group_rows), 1)
    mover = (cols_of == (rows_of % ROWS) * channels + rows_of // ROWS).astype(BF16)
    eye = (
        lax.broadcasted_iota(jnp.int32, (kept, kept), 0) == lax.broadcasted_iota(jnp.int32, (kept, kept), 1)
    ).astype(BF16)
    mask_cols = lax.dot_general(
        eye, mask_ref[...].astype(F32).astype(BF16), (((1,), (1,)), ((), ())), preferred_element_type=F32
    )
    for g in range(kept // ROWS):
        rows = tmpl_ref[pl.ds(g * group_rows, group_rows), :]
        turned_rows = jnp.concatenate(
            [
                jnp.dot(rows[:, :half], flip, preferred_element_type=F32),
                jnp.dot(rows[:, half:], flip, preferred_element_type=F32),
            ],
            axis=1,
        ).astype(BF16)
        moved = jnp.dot(mover, turned_rows, preferred_element_type=F32)
        for c in range(channels):
            block = moved[c * ROWS : (c + 1) * ROWS]
            square = jnp.sum(block * block, axis=1, keepdims=True)
            weight = mask_cols[g * ROWS : (g + 1) * ROWS, c : c + 1] * lax.rsqrt(square + 1e-6)
            normed_buf[c, pl.ds(g * ROWS, ROWS), :] = (block * weight).astype(BF16)

    def arrive(r):
        @pl.when(r != me)
        def _():
            pay_copy(0, r, r, seg).wait_recv()

        @pl.when(seg < segs - 1)
        def _():
            pay_copy(1, r, r, seg).wait_recv()

    each(regions, arrive)

    flag_row = components * pieces
    before = jnp.zeros((1, LANES), F32)
    first = [jnp.zeros((ROWS, LANES), F32) for _ in range(capacity)]
    second = [jnp.zeros((ROWS, LANES), F32) for _ in range(capacity)]
    filled = [jnp.zeros((1, LANES), F32) for _ in range(capacity)]
    for r in range(regions):
        here = got_buf[0, r].astype(F32)
        later = got_buf[1, r].astype(F32)
        present = here[flag_row : flag_row + 1, :]
        for j in range(min(capacity, r + 1)):
            chosen = jnp.where(before == float(j), present, 0.0)
            first[j] = first[j] + here * chosen
            second[j] = second[j] + later * chosen
            filled[j] = filled[j] + chosen
        before = before + present
    now = jnp.concatenate(first, axis=0)
    following = jnp.concatenate(second, axis=0)
    own_buf[0] = now
    own_buf[1] = following

    tri_row = lax.broadcasted_iota(jnp.int32, (LANES, LANES), 0)
    tri_col = lax.broadcasted_iota(jnp.int32, (LANES, LANES), 1)
    suffix_of = (tri_row >= tri_col).astype(BF16)
    prefix_of = (tri_row < tri_col).astype(BF16)
    every = jnp.ones((LANES, LANES), BF16)

    def exact_sums(values, sides):
        square = values * values
        high = square.astype(BF16)
        low = (square - high.astype(F32)).astype(BF16)
        return jnp.dot(high, sides, preferred_element_type=F32) + jnp.dot(low, sides, preferred_element_type=F32)

    now_sums = exact_sums(now, jnp.concatenate([suffix_of, every], axis=1))
    later_sums = exact_sums(following, jnp.concatenate([prefix_of, every], axis=1))
    energy = now_sums[:, :LANES] + later_sums[:, :LANES]
    tile_rows = capacity * ROWS
    place = lax.broadcasted_iota(jnp.int32, (tile_rows, LANES), 0) % pieces
    for d in range(1, pieces):
        ahead = pltpu.roll(now_sums[:, LANES:], tile_rows - d, 0)
        energy = energy + jnp.where(place + d < pieces, ahead, 0.0)
        behind = pltpu.roll(later_sums[:, LANES:], d, 0)
        energy = energy + jnp.where(place >= d, behind, 0.0)
    held = jnp.concatenate([jnp.broadcast_to(f, (ROWS, LANES)) for f in filled], axis=0)
    inv_buf[...] = held * lax.rsqrt(jnp.maximum(energy, 1.0))

    inside = tri_col <= tri_row
    strips = half // LANES
    spans = (taps // 2 + seg_len) // LANES

    def channel_windows(slot, c):
        def turned(w):
            piece = own_buf[w // pieces, pl.ds(slot * ROWS + c * pieces + w % pieces, 1), :]
            return pltpu.roll(
                jnp.broadcast_to(piece, (LANES, LANES)), 1, 1, stride=1, stride_axis=0
            )

        current = turned(0)
        for w in range(spans + strips - 1):
            upcoming = turned(w + 1)
            block = jnp.where(inside, current, upcoming).astype(BF16)
            for i in range(strips):
                if 0 <= w - i < spans:
                    first_row = (strips - 1 - i) * LANES
                    hankel_buf[c, first_row : first_row + LANES, (w - i) * LANES : (w - i + 1) * LANES] = block
            current = upcoming

    def one_slot(slot, stacked):
        for c in range(components):
            channel_windows(slot, c)
            normed = normed_buf[c * capacity + slot]
            product = jnp.dot(normed[:, :half], hankel_buf[c, :, :seg_len], preferred_element_type=F32)
            product = product + jnp.dot(
                normed[:, half:], hankel_buf[c, :, half : half + seg_len], preferred_element_type=F32
            )
            scales = [
                inv_buf[pl.ds(slot * ROWS + c * pieces + b, 1), :] for b in range(pieces)
            ]
            stacked = stacked + product * jnp.concatenate(scales, axis=1)
        return stacked

    stacked = jnp.zeros((kept, seg_len), F32)
    if capacity <= 4:
        for slot in range(capacity):
            stacked = one_slot(slot, stacked)
    else:
        stacked = lax.fori_loop(0, capacity, one_slot, stacked)

    chunk_rows = kept // chunks
    for q in range(chunks):
        part_buf[q] = stacked[q * chunk_rows : (q + 1) * chunk_rows].astype(BF16)

    def part_copy(q, slot):
        return pltpu.make_async_remote_copy(
            src_ref=part_buf.at[q],
            dst_ref=sums_buf.at[slot],
            send_sem=part_send.at[q],
            recv_sem=part_recv.at[slot],
            device_id={"region": q, "seg": seg},
            device_id_type=MESH,
        )

    def send_part(q):
        @pl.when(q != me)
        def _():
            part_copy(q, me).start()

    each(chunks, send_part)

    def gather_copy(r, slot):
        return pltpu.make_async_remote_copy(
            src_ref=mine_buf,
            dst_ref=gather_buf.at[slot],
            send_sem=gather_send.at[r],
            recv_sem=gather_recv.at[slot],
            device_id={"region": r, "seg": seg},
            device_id_type=MESH,
        )

    def power_copy(r, s, slot, slot_seg):
        return pltpu.make_async_remote_copy(
            src_ref=power_mine,
            dst_ref=power_buf.at[slot_seg, slot],
            send_sem=power_send.at[s, r],
            recv_sem=power_recv.at[slot_seg, slot],
            device_id={"region": r, "seg": s},
            device_id_type=MESH,
        )

    def not_me(index):
        r, s = index // segs, index % segs
        return r, s, (r != me) | (s != seg)

    @pl.when(me < chunks)
    def _():
        sums_buf[me] = part_buf[me]

        def take(r):
            @pl.when(r != me)
            def _():
                part_copy(0, r).wait_recv()

        each(regions, take)
        total = sums_buf[0].astype(F32)
        for r in range(1, regions):
            total = total + sums_buf[r].astype(F32)
        mine_buf[...] = total.astype(BF16)
        gather_buf[me] = mine_buf[...]
        power = jnp.sum(total * total, axis=1, keepdims=True)
        power_mine[...] = jnp.broadcast_to(power, power_mine.shape)
        power_buf[seg, me] = power_mine[...]

        def send_power(index):
            r, s, other = not_me(index)

            @pl.when(other)
            def _():
                power_copy(r, s, me, seg).start()

        def send_mine(r):
            @pl.when(r != me)
            def _():
                gather_copy(r, me).start()

        each(regions * segs, send_power)
        each(regions, send_mine)

    for q in range(chunks):
        for s in range(segs):
            @pl.when((q != me) | (s != seg))
            def _():
                power_copy(0, 0, q, s).wait_recv()

        @pl.when(q != me)
        def _():
            gather_copy(0, q).wait_recv()

        power = power_buf[0, q]
        for s in range(1, segs):
            power = power + power_buf[s, q]
        scale = lax.rsqrt(power / total_len + 1e-6)
        for b in range(pieces):
            span = slice(b * LANES, (b + 1) * LANES)
            out_ref[q * chunk_rows : (q + 1) * chunk_rows, span] = gather_buf[q, :, span].astype(F32) * scale

    def sent_records(r):
        @pl.when(r != me)
        def _():
            pay_copy(0, r, me, seg).wait_send()

        @pl.when(seg > 0)
        def _():
            pay_copy(1, r, me, seg).wait_send()

    each(regions, sent_records)

    def sent_part(q):
        @pl.when(q != me)
        def _():
            part_copy(q, me).wait_send()

    each(chunks, sent_part)

    @pl.when(me < chunks)
    def _():
        def sent_power(index):
            r, s, other = not_me(index)

            @pl.when(other)
            def _():
                power_copy(r, s, me, seg).wait_send()

        def sent_mine(r):
            @pl.when(r != me)
            def _():
                gather_copy(r, me).wait_send()

        each(regions * segs, sent_power)
        each(regions, sent_mine)


def per_device(mesh, records, templates, channel_mask, station_region):
    local_batches, kept, capacity, components, taps = templates.shape
    local_count, _, seg_len = records.shape
    regions, segs = mesh.shape["region"], mesh.shape["seg"]
    rows = local_batches * kept
    channels = capacity * components
    chunks = min(regions, rows // ROWS)
    chunk_rows = rows // chunks
    pieces = seg_len // LANES
    assert seg_len == taps and components * pieces < ROWS and local_batches == 1

    rec = records.transpose(1, 0, 2)
    tmpl = templates.transpose(0, 1, 3, 2, 4).reshape(rows * channels, taps)
    mask = channel_mask.transpose(0, 3, 2, 1).reshape(channels, rows)
    vmem = pl.BlockSpec(memory_space=pltpu.VMEM)
    dma = pltpu.SemaphoreType.DMA
    detect = pl.pallas_call(
        functools.partial(detect_kernel, regions, segs),
        out_shape=jax.ShapeDtypeStruct((rows, seg_len), F32),
        in_specs=[pl.BlockSpec(memory_space=pltpu.SMEM), vmem, vmem, vmem],
        out_specs=vmem,
        scratch_shapes=[
            pltpu.VMEM((local_count, ROWS, LANES), F32),
            pltpu.VMEM((regions, ROWS, LANES), BF16),
            pltpu.VMEM((2, regions, ROWS, LANES), BF16),
            pltpu.VMEM((2, capacity * ROWS, LANES), F32),
            pltpu.VMEM((capacity * ROWS, LANES), F32),
            pltpu.VMEM((channels, rows, taps), BF16),
            pltpu.VMEM((components, taps // 2, taps // 2 + seg_len), BF16),
            pltpu.VMEM((chunks, chunk_rows, seg_len), BF16),
            pltpu.VMEM((regions, chunk_rows, seg_len), BF16),
            pltpu.VMEM((chunk_rows, seg_len), BF16),
            pltpu.VMEM((chunks, chunk_rows, seg_len), BF16),
            pltpu.VMEM((chunk_rows, LANES), F32),
            pltpu.VMEM((segs, chunks, chunk_rows, LANES), F32),
            dma((2, regions)),
            dma((2, regions)),
            dma((chunks,)),
            dma((regions,)),
            dma((regions,)),
            dma((chunks,)),
            dma((segs, regions)),
            dma((segs, chunks)),
        ],
        compiler_params=pltpu.CompilerParams(
            collective_id=0, has_side_effects=True, vmem_limit_bytes=40 * 1024 * 1024
        ),
    )(station_region, rec, tmpl, mask)
    return detect.reshape(local_batches, kept, seg_len)


def solution(mesh):
    placed = (
        P(("groups", "region"), None, "seg"),
        P(("groups", "tb"), None, "region", None, None),
        P(("groups", "tb"), None, "region", None),
        P(("groups", "region")),
    )
    return jax.shard_map(
        functools.partial(per_device, mesh),
        mesh=mesh,
        in_specs=placed,
        out_specs=P(("groups", "tb"), None, "seg"),
        check_vma=False,
    )
```

```python
import functools

import jax
import jax.numpy as jnp
from jax import lax
from jax.experimental import pallas as pl
from jax.experimental.pallas import tpu as pltpu
from jax.sharding import PartitionSpec as P

MESH = pl.DeviceIdType.MESH
LANES = 128
ROWS = 16
F32 = jnp.float32
BF16 = jnp.bfloat16


def each(count, body):
    if count <= 8:
        for index in range(count):
            body(index)
    else:
        def step(index, carry):
            body(index)
            return carry

        lax.fori_loop(0, count, step, 0)


def detect_kernel(
    regions,
    segs,
    region_hbm,
    rec_hbm,
    tmpl_hbm,
    mask_hbm,
    out_ref,
    region_ref,
    rec_ref,
    tmpl_ref,
    mask_ref,
    station_buf,
    pay_buf,
    got_buf,
    own_buf,
    inv_buf,
    normed_buf,
    hankel_buf,
    part_buf,
    sums_buf,
    mine_buf,
    gather_buf,
    power_buf,
    load_sem,
    pay_send,
    pay_recv,
    part_send,
    part_recv,
    gather_send,
    gather_recv,
    power_send,
    power_recv,
):
    components, local_count, seg_len = rec_ref.shape
    channels, _, kept, half = normed_buf.shape
    taps = 2 * half
    capacity = channels // components
    pieces = seg_len // LANES
    chunks = part_buf.shape[0]
    total_len = seg_len * segs
    me = lax.axis_index("region")
    seg = lax.axis_index("seg")

    loads = [
        pltpu.make_async_copy(source, target, load_sem.at[index])
        for index, (source, target) in enumerate(
            ((region_hbm, region_ref), (rec_hbm, rec_ref), (mask_hbm, mask_ref), (tmpl_hbm, tmpl_ref))
        )
    ]
    for load in loads:
        load.start()
    barrier = pltpu.get_barrier_semaphore()

    def peer_region(d):
        return lax.rem(me + d, regions)

    def peer_seg(e):
        return lax.rem(seg + e, segs)

    def other_peer(index):
        r, s = peer_region((index + 1) // segs), peer_seg((index + 1) % segs)
        return r, s

    def greet(index):
        r, s = other_peer(index)
        pl.semaphore_signal(barrier, inc=1, device_id={"region": r, "seg": s}, device_id_type=MESH)

    each(regions * segs - 1, greet)

    station_buf[...] = jnp.ones_like(station_buf)
    loads[0].wait()
    loads[1].wait()
    for c in range(components):
        samples = rec_ref[c].astype(F32)
        for n in range(local_count):
            for j in range(pieces):
                station_buf[n, pl.ds(c * pieces + j, 1), :] = samples[n : n + 1, j * LANES : (j + 1) * LANES]

    def fill(r):
        total = jnp.zeros((ROWS, LANES), F32)
        for n in range(local_count):
            total = total + station_buf[n] * (region_ref[n] == r).astype(F32)
        pay_buf[r] = total.astype(BF16)

    each(regions, fill)
    got_buf[0, me] = pay_buf[me]

    pl.semaphore_wait(barrier, regions * segs - 1)

    def pay_copy(which, r, slot, target_seg):
        return pltpu.make_async_remote_copy(
            src_ref=pay_buf.at[r],
            dst_ref=got_buf.at[which, slot],
            send_sem=pay_send.at[which, r],
            recv_sem=pay_recv.at[which, slot],
            device_id={"region": r, "seg": target_seg},
            device_id_type=MESH,
        )

    earlier_seg = peer_seg(segs - 1)

    def send_records(d):
        r = peer_region(regions - 1 - d)
        pay_copy(1, r, me, earlier_seg).start()
        if isinstance(d, int):
            if d < regions - 1:
                pay_copy(0, r, me, seg).start()
        else:
            @pl.when(d < regions - 1)
            def _():
                pay_copy(0, r, me, seg).start()

    each(regions, send_records)

    loads[2].wait()
    loads[3].wait()
    flip_row = lax.broadcasted_iota(jnp.int32, (half, half), 0)
    flip_col = lax.broadcasted_iota(jnp.int32, (half, half), 1)
    flip = (flip_row + flip_col == half - 1).astype(BF16)
    group_rows = ROWS * channels
    rows_of = lax.broadcasted_iota(jnp.int32, (group_rows, group_rows), 0)
    cols_of = lax.broadcasted_iota(jnp.int32, (group_rows, group_rows), 1)
    mover = (cols_of == (rows_of % ROWS) * channels + rows_of // ROWS).astype(BF16)
    eye = (
        lax.broadcasted_iota(jnp.int32, (kept, kept), 0) == lax.broadcasted_iota(jnp.int32, (kept, kept), 1)
    ).astype(BF16)
    mask_cols = [
        lax.dot_general(
            eye, mask_ref[c].astype(F32).astype(BF16), (((1,), (1,)), ((), ())), preferred_element_type=F32
        )
        for c in range(components)
    ]
    for g in range(kept // ROWS):
        rows = tmpl_ref[pl.ds(g * ROWS * components, ROWS * components)].reshape(group_rows, taps)
        turned_rows = jnp.concatenate(
            [
                jnp.dot(rows[:, :half], flip, preferred_element_type=F32),
                jnp.dot(rows[:, half:], flip, preferred_element_type=F32),
            ],
            axis=1,
        ).astype(BF16)
        moved = jnp.dot(mover, turned_rows, preferred_element_type=F32)
        for c in range(channels):
            block = moved[c * ROWS : (c + 1) * ROWS]
            square = jnp.sum(block * block, axis=1, keepdims=True)
            slot = c % capacity
            mask = mask_cols[c // capacity][g * ROWS : (g + 1) * ROWS, slot : slot + 1]
            normed = (block * (mask * lax.rsqrt(square + 1e-6))).astype(BF16)
            normed_buf[c, 0, pl.ds(g * ROWS, ROWS), :] = normed[:, :half]
            normed_buf[c, 1, pl.ds(g * ROWS, ROWS), :] = normed[:, half:]

    def arrive(d):
        r = peer_region(d + 1)
        pay_copy(1, r, r, earlier_seg).wait_recv()
        if isinstance(d, int):
            if d < regions - 1:
                pay_copy(0, r, r, seg).wait_recv()
        else:
            @pl.when(d < regions - 1)
            def _():
                pay_copy(0, r, r, seg).wait_recv()

    each(regions, arrive)

    flag_row = components * pieces
    before = jnp.zeros((1, LANES), F32)
    first = [jnp.zeros((ROWS, LANES), F32) for _ in range(capacity)]
    second = [jnp.zeros((ROWS, LANES), F32) for _ in range(capacity)]
    filled = [jnp.zeros((1, LANES), F32) for _ in range(capacity)]
    for r in range(regions):
        here = got_buf[0, r].astype(F32)
        later = got_buf[1, r].astype(F32)
        present = here[flag_row : flag_row + 1, :]
        for j in range(min(capacity, r + 1)):
            chosen = jnp.where(before == float(j), present, 0.0)
            first[j] = first[j] + here * chosen
            second[j] = second[j] + later * chosen
            filled[j] = filled[j] + chosen
        before = before + present
    now = jnp.concatenate(first, axis=0)
    following = jnp.concatenate(second, axis=0) * (seg < segs - 1).astype(F32)
    own_buf[0] = now
    own_buf[1] = following

    tri_row = lax.broadcasted_iota(jnp.int32, (LANES, LANES), 0)
    tri_col = lax.broadcasted_iota(jnp.int32, (LANES, LANES), 1)
    suffix_of = (tri_row >= tri_col).astype(BF16)
    prefix_of = (tri_row < tri_col).astype(BF16)
    every = jnp.ones((LANES, LANES), BF16)

    def exact_sums(values, sides):
        square = values * values
        high = square.astype(BF16)
        low = (square - high.astype(F32)).astype(BF16)
        return jnp.dot(high, sides, preferred_element_type=F32) + jnp.dot(low, sides, preferred_element_type=F32)

    now_sums = exact_sums(now, jnp.concatenate([suffix_of, every], axis=1))
    later_sums = exact_sums(following, jnp.concatenate([prefix_of, every], axis=1))
    energy = now_sums[:, :LANES] + later_sums[:, :LANES]
    tile_rows = capacity * ROWS
    place = lax.broadcasted_iota(jnp.int32, (tile_rows, LANES), 0) % pieces
    for d in range(1, pieces):
        ahead = pltpu.roll(now_sums[:, LANES:], tile_rows - d, 0)
        energy = energy + jnp.where(place + d < pieces, ahead, 0.0)
        behind = pltpu.roll(later_sums[:, LANES:], d, 0)
        energy = energy + jnp.where(place >= d, behind, 0.0)
    held = jnp.concatenate([jnp.broadcast_to(f, (ROWS, LANES)) for f in filled], axis=0)
    inv_buf[...] = held * lax.rsqrt(jnp.maximum(energy, 1.0))

    inside = tri_col <= tri_row
    strips = half // LANES
    spans = (taps // 2 + seg_len) // LANES

    def channel_windows(slot, c):
        def turned(w):
            piece = own_buf[w // pieces, pl.ds(slot * ROWS + c * pieces + w % pieces, 1), :]
            return pltpu.roll(
                jnp.broadcast_to(piece, (LANES, LANES)), 1, 1, stride=1, stride_axis=0
            )

        current = turned(0)
        for w in range(spans + strips - 1):
            upcoming = turned(w + 1)
            block = jnp.where(inside, current, upcoming).astype(BF16)
            for i in range(strips):
                if 0 <= w - i < spans:
                    first_row = (strips - 1 - i) * LANES
                    hankel_buf[c, first_row : first_row + LANES, (w - i) * LANES : (w - i + 1) * LANES] = block
            current = upcoming

    def one_slot(slot, stacked):
        for c in range(components):
            channel_windows(slot, c)
            normed = normed_buf[c * capacity + slot]
            early = jnp.dot(normed[0], hankel_buf[c, :, :half], preferred_element_type=F32)
            middle = jnp.dot(
                normed.reshape(2 * kept, half), hankel_buf[c, :, half : 2 * half], preferred_element_type=F32
            )
            late = jnp.dot(normed[1], hankel_buf[c, :, 2 * half :], preferred_element_type=F32)
            product = jnp.concatenate([early + middle[kept:], middle[:kept] + late], axis=1)
            scales = [
                inv_buf[pl.ds(slot * ROWS + c * pieces + b, 1), :] for b in range(pieces)
            ]
            stacked = stacked + product * jnp.concatenate(scales, axis=1)
        return stacked

    stacked = jnp.zeros((kept, seg_len), F32)
    if capacity <= 4:
        for slot in range(capacity):
            stacked = one_slot(slot, stacked)
    else:
        stacked = lax.fori_loop(0, capacity, one_slot, stacked)

    chunk_rows = kept // chunks
    for q in range(chunks):
        part_buf[q] = stacked[q * chunk_rows : (q + 1) * chunk_rows].astype(BF16)

    def part_copy(q, slot):
        return pltpu.make_async_remote_copy(
            src_ref=part_buf.at[q],
            dst_ref=sums_buf.at[slot],
            send_sem=part_send.at[q],
            recv_sem=part_recv.at[slot],
            device_id={"region": q, "seg": seg},
            device_id_type=MESH,
        )

    whole = chunks == regions

    def where_owner(condition, run):
        if whole:
            run()
        else:
            pl.when(condition)(run)

    def send_part(d):
        q = peer_region(regions - 1 - d)
        where_owner(q < chunks, lambda: part_copy(q, me).start())

    each(regions - 1, send_part)

    def gather_copy(r, slot):
        return pltpu.make_async_remote_copy(
            src_ref=mine_buf,
            dst_ref=gather_buf.at[slot],
            send_sem=gather_send.at[r],
            recv_sem=gather_recv.at[slot],
            device_id={"region": r, "seg": seg},
            device_id_type=MESH,
        )

    def power_copy(r, s, slot, slot_seg):
        return pltpu.make_async_remote_copy(
            src_ref=mine_buf.at[:, pl.ds(seg_len, LANES)],
            dst_ref=power_buf.at[slot_seg, slot],
            send_sem=power_send.at[s, r],
            recv_sem=power_recv.at[slot_seg, slot],
            device_id={"region": r, "seg": s},
            device_id_type=MESH,
        )

    def own_chunk():
        sums_buf[me] = part_buf[me]

        def take(d):
            part_copy(0, peer_region(d + 1)).wait_recv()

        each(regions - 1, take)
        total = sums_buf[0].astype(F32)
        for r in range(1, regions):
            total = total + sums_buf[r].astype(F32)
        mine_buf[:, :seg_len] = total.astype(BF16)
        power = jnp.broadcast_to(jnp.sum(total * total, axis=1, keepdims=True), (chunk_rows, LANES))
        high = power.astype(BF16).astype(F32)
        lanes = lax.broadcasted_iota(jnp.int32, (chunk_rows, LANES), 1)
        mine_buf[:, seg_len:] = jnp.where(lanes < LANES // 2, high, power - high).astype(BF16)

        def send_mine(d):
            gather_copy(peer_region(regions - 1 - d), me).start()

        def send_power(index):
            r, s = peer_region(index // (segs - 1) + 1), peer_seg(index % (segs - 1) + 1)
            power_copy(r, s, me, seg).start()

        each(regions - 1, send_mine)
        each(regions * (segs - 1), send_power)
        gather_buf[me] = mine_buf[...]

    where_owner(me < chunks, own_chunk)

    def finish(d):
        q = peer_region(d)
        where_owner(q < chunks, lambda: finish_chunk(q, d))

    def finish_chunk(q, d):
        if not isinstance(d, int):
            pl.when(d > 0)(lambda: gather_copy(0, q).wait_recv())
        elif d > 0:
            gather_copy(0, q).wait_recv()
        powers = gather_buf[q, :, seg_len:].astype(F32)
        for e in range(1, segs):
            s = peer_seg(e)
            power_copy(0, 0, q, s).wait_recv()
            powers = powers + power_buf[s, q].astype(F32)
        power = powers[:, :1] + powers[:, LANES // 2 : LANES // 2 + 1]
        scale = lax.rsqrt(power / total_len + 1e-6)
        out_ref[q] = gather_buf[q, :, :seg_len].astype(F32) * scale

    each(regions, finish)

    def sent_records(d):
        r = peer_region(d + 1)
        pay_copy(1, r, me, earlier_seg).wait_send()
        if isinstance(d, int):
            if d < regions - 1:
                pay_copy(0, r, me, seg).wait_send()
        else:
            @pl.when(d < regions - 1)
            def _():
                pay_copy(0, r, me, seg).wait_send()

    each(regions, sent_records)

    def sent_part(d):
        q = peer_region(d + 1)
        where_owner(q < chunks, lambda: part_copy(q, me).wait_send())

    each(regions - 1, sent_part)

    def sent_chunk():
        def sent_power(index):
            r, s = peer_region(index // (segs - 1) + 1), peer_seg(index % (segs - 1) + 1)
            power_copy(r, s, me, seg).wait_send()

        each(regions * (segs - 1), sent_power)
        each(regions - 1, lambda d: gather_copy(peer_region(d + 1), me).wait_send())

    where_owner(me < chunks, sent_chunk)


def per_device(mesh, records, templates, channel_mask, station_region):
    local_batches, kept, capacity, components, taps = templates.shape
    local_count, _, seg_len = records.shape
    regions, segs = mesh.shape["region"], mesh.shape["seg"]
    rows = local_batches * kept
    channels = capacity * components
    chunks = min(regions, rows // ROWS)
    chunk_rows = rows // chunks
    pieces = seg_len // LANES
    assert seg_len == taps and components * pieces < ROWS and local_batches == 1

    rec = records.transpose(1, 0, 2)
    tmpl = templates.transpose(0, 1, 3, 2, 4).reshape(rows * components, capacity, taps)
    mask = channel_mask.transpose(0, 3, 2, 1).reshape(components, capacity, rows)
    in_hbm = pl.BlockSpec(memory_space=pltpu.HBM)
    dma = pltpu.SemaphoreType.DMA
    detect = pl.pallas_call(
        functools.partial(detect_kernel, regions, segs),
        out_shape=jax.ShapeDtypeStruct((chunks, chunk_rows, seg_len), F32),
        in_specs=[in_hbm] * 4,
        out_specs=pl.BlockSpec(memory_space=pltpu.VMEM),
        scratch_shapes=[
            pltpu.SMEM(station_region.shape, jnp.int32),
            pltpu.VMEM(rec.shape, BF16),
            pltpu.VMEM(tmpl.shape, BF16),
            pltpu.VMEM(mask.shape, jnp.int32),
            pltpu.VMEM((local_count, ROWS, LANES), F32),
            pltpu.VMEM((regions, ROWS, LANES), BF16),
            pltpu.VMEM((2, regions, ROWS, LANES), BF16),
            pltpu.VMEM((2, capacity * ROWS, LANES), F32),
            pltpu.VMEM((capacity * ROWS, LANES), F32),
            pltpu.VMEM((channels, 2, rows, taps // 2), BF16),
            pltpu.VMEM((components, taps // 2, taps // 2 + seg_len), BF16),
            pltpu.VMEM((chunks, chunk_rows, seg_len), BF16),
            pltpu.VMEM((regions, chunk_rows, seg_len), BF16),
            pltpu.VMEM((chunk_rows, seg_len + LANES), BF16),
            pltpu.VMEM((chunks, chunk_rows, seg_len + LANES), BF16),
            pltpu.VMEM((segs, chunks, chunk_rows, LANES), BF16),
            dma((4,)),
            dma((2, regions)),
            dma((2, regions)),
            dma((chunks,)),
            dma((regions,)),
            dma((regions,)),
            dma((chunks,)),
            dma((segs, regions)),
            dma((segs, chunks)),
        ],
        compiler_params=pltpu.CompilerParams(
            collective_id=0, has_side_effects=True, vmem_limit_bytes=62 * 1024 * 1024
        ),
    )(station_region, rec, tmpl, mask)
    return detect.reshape(local_batches, kept, seg_len)


def solution(mesh):
    placed = (
        P(("groups", "region"), None, "seg"),
        P(("groups", "tb"), None, "region", None, None),
        P(("groups", "tb"), None, "region", None),
        P(("groups", "region")),
    )
    return jax.shard_map(
        functools.partial(per_device, mesh),
        mesh=mesh,
        in_specs=placed,
        out_specs=P(("groups", "tb"), None, "seg"),
        check_vma=False,
    )
```

```python
import functools

import jax
import jax.numpy as jnp
from jax import lax
from jax.experimental import pallas as pl
from jax.experimental.pallas import tpu as pltpu
from jax.sharding import PartitionSpec as P

MESH = pl.DeviceIdType.MESH
LANES = 128
ROWS = 16
F32 = jnp.float32
BF16 = jnp.bfloat16


def each(count, body):
    if count <= 8:
        for index in range(count):
            body(index)
    else:
        def step(index, carry):
            body(index)
            return carry

        lax.fori_loop(0, count, step, 0)


def detect_kernel(
    regions,
    segs,
    region_hbm,
    rec_hbm,
    tmpl_hbm,
    mask_hbm,
    out_ref,
    region_ref,
    rec_ref,
    tmpl_ref,
    mask_ref,
    station_buf,
    pay_buf,
    got_buf,
    own_buf,
    inv_buf,
    normed_buf,
    hankel_buf,
    part_buf,
    sums_buf,
    mine_buf,
    gather_buf,
    power_buf,
    load_sem,
    pay_send,
    pay_recv,
    part_send,
    part_recv,
    gather_send,
    gather_recv,
    power_send,
    power_recv,
):
    components, local_count, seg_len = rec_ref.shape
    channels, _, kept, half = normed_buf.shape
    taps = 2 * half
    capacity = channels // components
    pieces = seg_len // LANES
    chunks = part_buf.shape[0]
    total_len = seg_len * segs
    me = lax.axis_index("region")
    seg = lax.axis_index("seg")

    loads = [
        pltpu.make_async_copy(source, target, load_sem.at[index])
        for index, (source, target) in enumerate(
            ((region_hbm, region_ref), (rec_hbm, rec_ref), (mask_hbm, mask_ref), (tmpl_hbm, tmpl_ref))
        )
    ]
    for load in loads:
        load.start()
    barrier = pltpu.get_barrier_semaphore()

    def peer_region(d):
        return lax.rem(me + d, regions)

    def peer_seg(e):
        return lax.rem(seg + e, segs)

    def other_peer(index):
        r, s = peer_region((index + 1) // segs), peer_seg((index + 1) % segs)
        return r, s

    def greet(index):
        r, s = other_peer(index)
        pl.semaphore_signal(barrier, inc=1, device_id={"region": r, "seg": s}, device_id_type=MESH)

    each(regions * segs - 1, greet)

    station_buf[...] = jnp.ones_like(station_buf)
    loads[0].wait()
    loads[1].wait()
    for c in range(components):
        samples = rec_ref[c].astype(F32)
        for n in range(local_count):
            for j in range(pieces):
                station_buf[n, pl.ds(c * pieces + j, 1), :] = samples[n : n + 1, j * LANES : (j + 1) * LANES]

    def fill(r):
        total = jnp.zeros((ROWS, LANES), F32)
        for n in range(local_count):
            total = total + station_buf[n] * (region_ref[n] == r).astype(F32)
        pay_buf[r] = total.astype(BF16)

    each(regions, fill)
    got_buf[0, me] = pay_buf[me]

    pl.semaphore_wait(barrier, regions * segs - 1)

    def pay_copy(which, r, slot, target_seg):
        return pltpu.make_async_remote_copy(
            src_ref=pay_buf.at[r],
            dst_ref=got_buf.at[which, slot],
            send_sem=pay_send.at[which, r],
            recv_sem=pay_recv.at[which, slot],
            device_id={"region": r, "seg": target_seg},
            device_id_type=MESH,
        )

    earlier_seg = peer_seg(segs - 1)

    def send_records(d):
        r = peer_region(regions - 1 - d)
        pay_copy(1, r, me, earlier_seg).start()
        if isinstance(d, int):
            if d < regions - 1:
                pay_copy(0, r, me, seg).start()
        else:
            @pl.when(d < regions - 1)
            def _():
                pay_copy(0, r, me, seg).start()

    each(regions, send_records)

    loads[2].wait()
    loads[3].wait()
    flip_row = lax.broadcasted_iota(jnp.int32, (half, half), 0)
    flip_col = lax.broadcasted_iota(jnp.int32, (half, half), 1)
    flip = (flip_row + flip_col == half - 1).astype(BF16)
    group_rows = ROWS * channels
    rows_of = lax.broadcasted_iota(jnp.int32, (group_rows, group_rows), 0)
    cols_of = lax.broadcasted_iota(jnp.int32, (group_rows, group_rows), 1)
    mover = (cols_of == (rows_of % ROWS) * channels + rows_of // ROWS).astype(BF16)
    eye = (
        lax.broadcasted_iota(jnp.int32, (kept, kept), 0) == lax.broadcasted_iota(jnp.int32, (kept, kept), 1)
    ).astype(BF16)
    mask_cols = [
        lax.dot_general(
            eye, mask_ref[c].astype(F32).astype(BF16), (((1,), (1,)), ((), ())), preferred_element_type=F32
        )
        for c in range(components)
    ]
    for g in range(kept // ROWS):
        rows = tmpl_ref[pl.ds(g * ROWS * components, ROWS * components)].reshape(group_rows, taps)
        turned_rows = jnp.concatenate(
            [
                jnp.dot(rows[:, :half], flip, preferred_element_type=F32),
                jnp.dot(rows[:, half:], flip, preferred_element_type=F32),
            ],
            axis=1,
        ).astype(BF16)
        moved = jnp.dot(mover, turned_rows, preferred_element_type=F32)
        for c in range(channels):
            block = moved[c * ROWS : (c + 1) * ROWS]
            square = jnp.sum(block * block, axis=1, keepdims=True)
            slot = c % capacity
            mask = mask_cols[c // capacity][g * ROWS : (g + 1) * ROWS, slot : slot + 1]
            normed = (block * (mask * lax.rsqrt(square + 1e-6))).astype(BF16)
            normed_buf[c, 0, pl.ds(g * ROWS, ROWS), :] = normed[:, :half]
            normed_buf[c, 1, pl.ds(g * ROWS, ROWS), :] = normed[:, half:]

    def arrive(d):
        r = peer_region(d + 1)
        pay_copy(1, r, r, earlier_seg).wait_recv()
        if isinstance(d, int):
            if d < regions - 1:
                pay_copy(0, r, r, seg).wait_recv()
        else:
            @pl.when(d < regions - 1)
            def _():
                pay_copy(0, r, r, seg).wait_recv()

    each(regions, arrive)

    flag_row = components * pieces
    before = jnp.zeros((1, LANES), F32)
    first = [jnp.zeros((ROWS, LANES), F32) for _ in range(capacity)]
    second = [jnp.zeros((ROWS, LANES), F32) for _ in range(capacity)]
    filled = [jnp.zeros((1, LANES), F32) for _ in range(capacity)]
    for r in range(regions):
        here = got_buf[0, r].astype(F32)
        later = got_buf[1, r].astype(F32)
        present = here[flag_row : flag_row + 1, :]
        for j in range(min(capacity, r + 1)):
            chosen = jnp.where(before == float(j), present, 0.0)
            first[j] = first[j] + here * chosen
            second[j] = second[j] + later * chosen
            filled[j] = filled[j] + chosen
        before = before + present
    now = jnp.concatenate(first, axis=0)
    following = jnp.concatenate(second, axis=0) * (seg < segs - 1).astype(F32)
    own_buf[0] = now
    own_buf[1] = following

    tri_row = lax.broadcasted_iota(jnp.int32, (LANES, LANES), 0)
    tri_col = lax.broadcasted_iota(jnp.int32, (LANES, LANES), 1)
    suffix_of = (tri_row >= tri_col).astype(BF16)
    prefix_of = (tri_row < tri_col).astype(BF16)
    every = jnp.ones((LANES, LANES), BF16)

    def exact_sums(values, sides):
        square = values * values
        high = square.astype(BF16)
        low = (square - high.astype(F32)).astype(BF16)
        return jnp.dot(high, sides, preferred_element_type=F32) + jnp.dot(low, sides, preferred_element_type=F32)

    now_sums = exact_sums(now, jnp.concatenate([suffix_of, every], axis=1))
    later_sums = exact_sums(following, jnp.concatenate([prefix_of, every], axis=1))
    energy = now_sums[:, :LANES] + later_sums[:, :LANES]
    tile_rows = capacity * ROWS
    place = lax.broadcasted_iota(jnp.int32, (tile_rows, LANES), 0) % pieces
    for d in range(1, pieces):
        ahead = pltpu.roll(now_sums[:, LANES:], tile_rows - d, 0)
        energy = energy + jnp.where(place + d < pieces, ahead, 0.0)
        behind = pltpu.roll(later_sums[:, LANES:], d, 0)
        energy = energy + jnp.where(place >= d, behind, 0.0)
    held = jnp.concatenate([jnp.broadcast_to(f, (ROWS, LANES)) for f in filled], axis=0)
    inv_buf[...] = held * lax.rsqrt(jnp.maximum(energy, 1.0))

    inside = tri_col <= tri_row
    strips = half // LANES
    spans = (taps // 2 + seg_len) // LANES

    def channel_windows(slot, c):
        def turned(w):
            piece = own_buf[w // pieces, pl.ds(slot * ROWS + c * pieces + w % pieces, 1), :]
            return pltpu.roll(
                jnp.broadcast_to(piece, (LANES, LANES)), 1, 1, stride=1, stride_axis=0
            )

        current = turned(0)
        for w in range(spans + strips - 1):
            upcoming = turned(w + 1)
            block = jnp.where(inside, current, upcoming).astype(BF16)
            for i in range(strips):
                if 0 <= w - i < spans:
                    first_row = (strips - 1 - i) * LANES
                    hankel_buf[c, first_row : first_row + LANES, (w - i) * LANES : (w - i + 1) * LANES] = block
            current = upcoming

    def one_slot(slot, stacked):
        for c in range(components):
            channel_windows(slot, c)
            normed = normed_buf[c * capacity + slot]
            early = jnp.dot(normed[0], hankel_buf[c, :, :half], preferred_element_type=F32)
            middle = jnp.dot(
                normed.reshape(2 * kept, half), hankel_buf[c, :, half : 2 * half], preferred_element_type=F32
            )
            late = jnp.dot(normed[1], hankel_buf[c, :, 2 * half :], preferred_element_type=F32)
            product = jnp.concatenate([early + middle[kept:], middle[:kept] + late], axis=1)
            scales = [
                inv_buf[pl.ds(slot * ROWS + c * pieces + b, 1), :] for b in range(pieces)
            ]
            stacked = stacked + product * jnp.concatenate(scales, axis=1)
        return stacked

    stacked = jnp.zeros((kept, seg_len), F32)
    if capacity <= 4:
        for slot in range(capacity):
            stacked = one_slot(slot, stacked)
    else:
        stacked = lax.fori_loop(0, capacity, one_slot, stacked)

    chunk_rows = kept // chunks
    for q in range(chunks):
        part_buf[q] = stacked[q * chunk_rows : (q + 1) * chunk_rows].astype(BF16)

    def part_copy(q, slot):
        return pltpu.make_async_remote_copy(
            src_ref=part_buf.at[q],
            dst_ref=sums_buf.at[slot],
            send_sem=part_send.at[q],
            recv_sem=part_recv.at[slot],
            device_id={"region": q, "seg": seg},
            device_id_type=MESH,
        )

    whole = chunks == regions

    def where_owner(condition, run):
        if whole:
            run()
        else:
            pl.when(condition)(run)

    def send_part(d):
        q = peer_region(regions - 1 - d)
        where_owner(q < chunks, lambda: part_copy(q, me).start())

    each(regions - 1, send_part)

    def gather_copy(r, slot):
        return pltpu.make_async_remote_copy(
            src_ref=mine_buf,
            dst_ref=gather_buf.at[slot],
            send_sem=gather_send.at[r],
            recv_sem=gather_recv.at[slot],
            device_id={"region": r, "seg": seg},
            device_id_type=MESH,
        )

    def power_copy(r, s, slot, slot_seg):
        return pltpu.make_async_remote_copy(
            src_ref=mine_buf.at[:, pl.ds(seg_len, LANES)],
            dst_ref=power_buf.at[slot_seg, slot],
            send_sem=power_send.at[s, r],
            recv_sem=power_recv.at[slot_seg, slot],
            device_id={"region": r, "seg": s},
            device_id_type=MESH,
        )

    def own_chunk():
        sums_buf[me] = part_buf[me]

        def take(d):
            part_copy(0, peer_region(d + 1)).wait_recv()

        each(regions - 1, take)
        total = sums_buf[0].astype(F32)
        for r in range(1, regions):
            total = total + sums_buf[r].astype(F32)
        mine_buf[:, :seg_len] = total.astype(BF16)
        power = jnp.broadcast_to(jnp.sum(total * total, axis=1, keepdims=True), (chunk_rows, LANES))
        high = power.astype(BF16).astype(F32)
        lanes = lax.broadcasted_iota(jnp.int32, (chunk_rows, LANES), 1)
        mine_buf[:, seg_len:] = jnp.where(lanes < LANES // 2, high, power - high).astype(BF16)

        def send_mine(d):
            gather_copy(peer_region(regions - 1 - d), me).start()

        def send_power(index):
            r, s = peer_region(index // (segs - 1) + 1), peer_seg(index % (segs - 1) + 1)
            power_copy(r, s, me, seg).start()

        each(regions - 1, send_mine)
        each(regions * (segs - 1), send_power)
        gather_buf[me] = mine_buf[...]

    where_owner(me < chunks, own_chunk)

    def finish(d):
        q = peer_region(d)
        where_owner(q < chunks, lambda: finish_chunk(q, d))

    def finish_chunk(q, d):
        if not isinstance(d, int):
            pl.when(d > 0)(lambda: gather_copy(0, q).wait_recv())
        elif d > 0:
            gather_copy(0, q).wait_recv()
        powers = gather_buf[q, :, seg_len:].astype(F32)
        for e in range(1, segs):
            s = peer_seg(e)
            power_copy(0, 0, q, s).wait_recv()
            powers = powers + power_buf[s, q].astype(F32)
        power = powers[:, :1] + powers[:, LANES // 2 : LANES // 2 + 1]
        scale = lax.rsqrt(power / total_len + 1e-6)
        out_ref[q] = gather_buf[q, :, :seg_len].astype(F32) * scale

    each(regions, finish)

    def sent_records(d):
        r = peer_region(d + 1)
        pay_copy(1, r, me, earlier_seg).wait_send()
        if isinstance(d, int):
            if d < regions - 1:
                pay_copy(0, r, me, seg).wait_send()
        else:
            @pl.when(d < regions - 1)
            def _():
                pay_copy(0, r, me, seg).wait_send()

    each(regions, sent_records)

    def sent_part(d):
        q = peer_region(d + 1)
        where_owner(q < chunks, lambda: part_copy(q, me).wait_send())

    each(regions - 1, sent_part)

    def sent_chunk():
        def sent_power(index):
            r, s = peer_region(index // (segs - 1) + 1), peer_seg(index % (segs - 1) + 1)
            power_copy(r, s, me, seg).wait_send()

        each(regions * (segs - 1), sent_power)
        each(regions - 1, lambda d: gather_copy(peer_region(d + 1), me).wait_send())

    where_owner(me < chunks, sent_chunk)


def per_device(mesh, records, templates, channel_mask, station_region):
    local_batches, kept, capacity, components, taps = templates.shape
    local_count, _, seg_len = records.shape
    regions, segs = mesh.shape["region"], mesh.shape["seg"]
    rows = local_batches * kept
    channels = capacity * components
    chunks = min(regions, rows // ROWS)
    chunk_rows = rows // chunks
    pieces = seg_len // LANES
    assert seg_len == taps and components * pieces < ROWS and local_batches == 1

    rec = records.transpose(1, 0, 2)
    tmpl = templates.transpose(0, 1, 3, 2, 4).reshape(rows * components, capacity, taps)
    mask = channel_mask.transpose(0, 3, 2, 1).reshape(components, capacity, rows)
    in_hbm = pl.BlockSpec(memory_space=pltpu.HBM)
    dma = pltpu.SemaphoreType.DMA
    detect = pl.pallas_call(
        functools.partial(detect_kernel, regions, segs),
        out_shape=jax.ShapeDtypeStruct((chunks, chunk_rows, seg_len), F32),
        in_specs=[in_hbm] * 4,
        out_specs=pl.BlockSpec(memory_space=pltpu.VMEM),
        scratch_shapes=[
            pltpu.SMEM(station_region.shape, jnp.int32),
            pltpu.VMEM(rec.shape, BF16),
            pltpu.VMEM(tmpl.shape, BF16),
            pltpu.VMEM(mask.shape, jnp.int32),
            pltpu.VMEM((local_count, ROWS, LANES), F32),
            pltpu.VMEM((regions, ROWS, LANES), BF16),
            pltpu.VMEM((2, regions, ROWS, LANES), BF16),
            pltpu.VMEM((2, capacity * ROWS, LANES), F32),
            pltpu.VMEM((capacity * ROWS, LANES), F32),
            pltpu.VMEM((channels, 2, rows, taps // 2), BF16),
            pltpu.VMEM((components, taps // 2, taps // 2 + seg_len), BF16),
            pltpu.VMEM((chunks, chunk_rows, seg_len), BF16),
            pltpu.VMEM((regions, chunk_rows, seg_len), BF16),
            pltpu.VMEM((chunk_rows, seg_len + LANES), BF16),
            pltpu.VMEM((chunks, chunk_rows, seg_len + LANES), BF16),
            pltpu.VMEM((segs, chunks, chunk_rows, LANES), BF16),
            dma((4,)),
            dma((2, regions)),
            dma((2, regions)),
            dma((chunks,)),
            dma((regions,)),
            dma((regions,)),
            dma((chunks,)),
            dma((segs, regions)),
            dma((segs, chunks)),
        ],
        compiler_params=pltpu.CompilerParams(
            collective_id=0, has_side_effects=True, vmem_limit_bytes=48 * 1024 * 1024
        ),
    )(*[pltpu.with_memory_space_constraint(operand, pltpu.HBM) for operand in (station_region, rec, tmpl, mask)])
    return detect.reshape(local_batches, kept, seg_len)


def solution(mesh):
    placed = (
        P(("groups", "region"), None, "seg"),
        P(("groups", "tb"), None, "region", None, None),
        P(("groups", "tb"), None, "region", None),
        P(("groups", "region")),
    )
    return jax.shard_map(
        functools.partial(per_device, mesh),
        mesh=mesh,
        in_specs=placed,
        out_specs=P(("groups", "tb"), None, "seg"),
        check_vma=False,
    )
```
